256 devices in a mesh: section: 2 (over z_lo), row: 16 (over x, y), col: 8 (over z_hi, core).
Axes of the slice: x: 4, y: 4, z: 8 (z_hi: 4, z_lo: 2; z = z_hi * 2 + z_lo), core: 2. Of those that a mesh axis runs over, the one named last changes fastest.
Arguments:
- section_hidden: bfloat16 [2, 1024, 28672], P('section', 'row', 'col'), may hold values from -6 to 6
- section_weight: bfloat16 [2, 28672, 8192], P('section', 'col', 'row'), may hold values from -0.046875 to 0.046875
- resid_in: bfloat16 [2, 1024, 8192], P('section', 'col', 'row'), may hold values from -40 to 40, as said below
- norm_gain: bfloat16 [8192], P('row'), may hold values from 0.25 to 1.75
Outputs:
- weight_grads: bfloat16 [2, 28672, 8192], P('section', 'col', 'row')
- section_out: bfloat16 [2, 1024, 28672], P('section', 'row', 'col')
The draws below stay inside these ranges and needn't reach their ends.
Inputs may be any that keep to these rules, and one draw needn't show every extreme that they name: `resid_in`: entries of order one with scales that differ from token to token and grow along the features.
All inputs are finite; a program needn't handle non-finite values.
Results may differ from the reference program's by a relative error of at most 0.0052.
Values may be sent and summed in bfloat16 or wider, within the bound.
A program may use at most 128 MiB of HBM per device.

```python
import math
import jax
import jax.numpy as jnp
from jax import lax

D = 8192
FF = 28672
TOKENS = 1024


def draw_resid_in(key, part):
    key = jax.random.fold_in(key, 7)
    key_tok, key_col, key_base = jax.random.split(key, 3)
    rising = 0.5 * jnp.exp(math.log(3.0) * jnp.arange(D, dtype=jnp.float32) / D)
    col_scale = rising[None, None, :] * jax.random.uniform(key_col, (2, 1, D), jnp.float32, 0.8, 1.25)
    tok_scale = jnp.exp(jax.random.uniform(key_tok, (2, TOKENS, 1), jnp.float32, math.log(0.4), math.log(4.0)))
    base_vals = jax.random.truncated_normal(key_base, -4.0, 4.0, (2, TOKENS, D), jnp.float32)
    return (base_vals * tok_scale * col_scale).astype(jnp.bfloat16)


def levels(key, shape, cuts, low, largest):
    def one(position, blocks):
        steps = jax.random.uniform(jax.random.fold_in(jax.random.fold_in(key, 6), position), (blocks,), jnp.float32, low / len(cuts), largest / len(cuts))
        return jnp.repeat(jnp.exp(steps), shape[position] // blocks).reshape((-1,) + (1,) * (len(shape) - position - 1))

    gain = one(*cuts[0])
    for cut in cuts[1:]:
        gain = gain * one(*cut)
    return gain


def centred(key, extent, spread, bound, cuts=(), kind=jnp.bfloat16):
    array = spread * jax.random.normal(key, extent, jnp.float32)
    if cuts:
        array = array * levels(key, extent, cuts, -0.22, 0.18)
    return jnp.clip(array, -bound, bound).astype(kind)


def setup_inputs(seed: int = 0) -> dict:
    arg_keys = jax.random.split(jax.random.key(seed), 5)
    return {
        "section_hidden": centred(arg_keys[0], (2, TOKENS, FF), 1.0, 6.0, ((0, 2), (1, 16), (2, 8))),
        "section_weight": centred(arg_keys[1], (2, FF, D), (2 * D) ** -0.5, 0.046875, ((0, 2), (1, 8), (2, 16))),
        "resid_in": draw_resid_in(jax.random.fold_in(arg_keys[4], 71), 0),
        "norm_gain": jnp.clip(1.0 + 0.15 * jax.random.normal(arg_keys[3], (D,), jnp.float32), 0.25, 1.75).astype(jnp.bfloat16),
    }


epsilon = 1e-05

def reference(section_hidden, section_weight, resid_in, norm_gain):
    hidden_a = section_hidden[0]
    grad_up = section_hidden[1]
    weight_a = section_weight[0]
    weight_b = section_weight[1]
    gain_f = norm_gain.astype(jnp.float32)
    sum_a = jnp.dot(hidden_a, weight_a, preferred_element_type=jnp.float32)
    layer_in = (resid_in[0].astype(jnp.float32) + sum_a).astype(jnp.bfloat16)
    grad_norm = jnp.dot(grad_up, weight_b, preferred_element_type=jnp.float32)
    layer_f = layer_in.astype(jnp.float32)
    sq_sum = lax.optimization_barrier(jnp.sum(layer_f * layer_f, axis=1, keepdims=True))
    cross_sum = lax.optimization_barrier(jnp.sum(grad_norm * gain_f * layer_f, axis=1, keepdims=True))
    inv_rms = lax.rsqrt(sq_sum / D + epsilon)
    normed = (layer_f * inv_rms * gain_f).astype(jnp.bfloat16)
    grad_in = (resid_in[1].astype(jnp.float32) + inv_rms * gain_f * grad_norm - layer_f * inv_rms ** 3 * (cross_sum / D)).astype(jnp.bfloat16)
    up_out = jnp.dot(normed, weight_b.T, preferred_element_type=jnp.float32).astype(jnp.bfloat16)
    grad_hidden = jnp.dot(grad_in, weight_a.T, preferred_element_type=jnp.float32).astype(jnp.bfloat16)
    grad_wa = jnp.dot(hidden_a.T, grad_in, preferred_element_type=jnp.float32).astype(jnp.bfloat16)
    grad_wb = jnp.dot(grad_up.T, normed, preferred_element_type=jnp.float32).astype(jnp.bfloat16)
    return (jnp.stack([grad_wa, grad_wb]), jnp.stack([grad_hidden, up_out]))
```

```python
import functools

import jax
import jax.numpy as jnp
from jax import lax
from jax.experimental import pallas as pl
from jax.experimental.pallas import tpu as pltpu
from jax.sharding import PartitionSpec as P

EPS = 1e-05
MESH = pl.DeviceIdType.MESH
F32 = jnp.float32
BF16 = jnp.bfloat16
K = 2
Q = 4
ALL = slice(None)


def mask_of(pos, mask):
    if mask == 1:
        return pos + 1 - 2 * lax.rem(pos, 2)
    if mask == 3:
        return 3 - pos
    return lax.rem(pos + 2, 4)


def gray(pos):
    high = lax.div(pos, 2)
    low = lax.rem(pos, 2)
    return high, high + low - 2 * high * low


def kernel(model_width, hidden, weight, resid, gain, grads, out, *scratch):
    (w, h, z, rc, rz1, rz2, own_resid, far_resid, swap_s, swap_r, ps_s, ps_x, ps_t, ps_y, x_, p2, r0, r1, r2, r3,
     outv, gv, l_w, l_h, l_r, l_o, l_g,
     ag_s, ag_r, rs_s, rs_r, zc_s, zc_r, z1_s, z1_r, z2_s, z2_r, q_s, q_r, sw_s, sw_r, px_s, px_r, py_s, py_r,
     x1_s, x1_r, x2_s, x2_r, xc_s, xc_r) = scratch
    rest = [r0, r1, r2, r3]
    tokens = hidden.shape[1] // K
    width = hidden.shape[2] // Q
    half = weight.shape[2] // 2
    sec = lax.axis_index("section")
    row = lax.axis_index("row")
    col = lax.axis_index("col")
    px, py = lax.div(row, 4), lax.rem(row, 4)
    zh, core = lax.div(col, 2), lax.rem(col, 2)
    gx1, gx0 = gray(px)
    gy1, gy0 = gray(py)
    gz1, gz0 = gray(zh)
    bits = [gx1, gx0, gy1, gy0]
    flips = [
        {"row": mask_of(px, 3) * 4 + py},
        {"row": mask_of(px, 1) * 4 + py},
        {"row": px * 4 + mask_of(py, 3)},
        {"row": px * 4 + mask_of(py, 1)},
    ]
    x_peers = [{"row": mask_of(px, m) * 4 + py} for m in (1, 2, 3)]
    y_peers = [{"row": px * 4 + mask_of(py, m)} for m in (1, 2, 3)]
    core_peer = {"col": zh * 2 + 1 - core}
    z_low = {"col": mask_of(zh, 1) * 2 + core}
    z_high = {"col": mask_of(zh, 3) * 2 + core}
    sec_peer = {"section": 1 - sec}

    barrier = pltpu.get_barrier_semaphore()
    partners = x_peers + y_peers + [core_peer, z_low, z_high, sec_peer]
    for peer in partners:
        pl.semaphore_signal(barrier, inc=1, device_id=peer, device_id_type=MESH)

    loads = []

    def load(src, dst, sem):
        copy = pltpu.make_async_copy(src, dst, sem)
        copy.start()
        return copy

    def own_block(k, q):
        return hidden.at[0, pl.ds(k * tokens, tokens), pl.ds(q * width, width)]

    h_loads = [[load(own_block(k, q), h.at[q, k, gx1, gx0, gy1, gy0], l_h.at[k, q]) for q in range(Q)] for k in range(K)]
    g_load = load(gain, gv, l_g)
    w_load = load(weight.at[0], w, l_w)
    start0 = pl.multiple_of(64 * core, 64)
    start1 = pl.multiple_of(64 * (1 - core), 64)
    r_loads = [
        [load(resid.at[0, pl.ds(start + k * tokens, tokens), :], own_resid.at[k, b], l_r.at[k, b]) for b, start in enumerate((start0, start1))]
        for k in range(K)
    ]

    pl.semaphore_wait(barrier, len(partners))

    sends = []

    def send(src, dst, ssem, rsem, peer):
        copy = pltpu.make_async_remote_copy(src, dst, ssem, rsem, device_id=peer, device_id_type=MESH)
        copy.start()
        sends.append(copy)
        return copy

    ag = {}

    def ag_index(q, i):
        free = {(q + n) % 4 for n in range(i)}
        return tuple(ALL if d in free else bits[d] for d in range(4))

    def ag_send(k, i):
        for q in range(Q):
            if i > 0:
                ag[k, q, i - 1].wait_recv()
            if i == 1:
                h_loads[k][q].wait()
            index = (q, k) + ag_index(q, i)
            src = own_block(k, q) if i == 0 else h.at[index]
            ag[k, q, i] = send(src, h.at[index], ag_s.at[k, q, i], ag_r.at[k, q, i], flips[(q + i) % 4])

    def ag_done(k):
        for q in range(Q):
            ag[k, q, 3].wait_recv()

    zc, z1, z2, sw, pxs, pys, x1, x2, xc, rs = {}, {}, {}, {}, {}, {}, {}, {}, {}, {}

    def first(k):
        if k == 0:
            w_load.wait()

        def tile(a):
            acc = None
            for q in range(Q):
                lhs = h[q, k, a].reshape(8 * tokens, width)
                term = jnp.dot(lhs, w[pl.ds(q * width, width), :], preferred_element_type=F32)
                acc = term if acc is None else acc + term
            for s in range(2):
                z[k, s, a] = acc[:, s * half : (s + 1) * half].reshape(2, 2, 2 * tokens, half)

        pl.loop(0, 2)(tile)
        zc[k] = send(z.at[k, :, :, :, 1 - core], rc.at[k], zc_s.at[k], zc_r.at[k], core_peer)

    def after_core(k):
        zc[k].wait_recv()
        z[k, :, :, :, core] = z[k, :, :, :, core] + rc[k]
        z1[k] = [
            send(z.at[k, 0, :, 1 - gz0, core], rz1.at[k, 0], z1_s.at[k, 0], z1_r.at[k, 0], z_low),
            send(z.at[k, 1, 1 - gz1, :, core], rz1.at[k, 1], z1_s.at[k, 1], z1_r.at[k, 1], z_high),
        ]

    def after_z1(k):
        z1[k][0].wait_recv()
        z[k, 0, :, gz0, core] = z[k, 0, :, gz0, core] + rz1[k, 0]
        first_half = send(z.at[k, 0, 1 - gz1, gz0, core], rz2.at[k, 0], z2_s.at[k, 0], z2_r.at[k, 0], z_high)
        z1[k][1].wait_recv()
        z[k, 1, gz1, :, core] = z[k, 1, gz1, :, core] + rz1[k, 1]
        z2[k] = [first_half, send(z.at[k, 1, gz1, 1 - gz0, core], rz2.at[k, 1], z2_s.at[k, 1], z2_r.at[k, 1], z_low)]

    def after_z2(k):
        for b in range(2):
            r_loads[k][b].wait()
        for s in range(2):
            z2[k][s].wait_recv()
            total = z[k, s, gz1, gz0, core] + rz2[k, s]
            res = own_resid[k, :, :, s * half : (s + 1) * half].reshape(2 * tokens, half).astype(F32)
            layer = (res + total).astype(BF16).astype(F32)
            swap_s[k, :, s * half : (s + 1) * half] = jnp.where(sec == 0, layer, total)
        sw[k] = send(swap_s.at[k], swap_r.at[k], sw_s.at[k], sw_r.at[k], sec_peer)

    def after_swap(k):
        if k == 0:
            g_load.wait()
        sw[k].wait_recv()
        mine, theirs = swap_s[k], swap_r[k]
        layer = jnp.where(sec == 0, mine, theirs)
        total = jnp.where(sec == 0, theirs, mine)
        gain_f = gv[...].astype(F32)
        squares = jnp.sum(layer * layer, axis=1, keepdims=True)
        cross = jnp.sum(total * gain_f * layer, axis=1, keepdims=True)
        lane = lax.broadcasted_iota(jnp.int32, (2 * tokens, 128), 1)
        ps_s[k] = jnp.where(lane < 64, squares, cross)
        pxs[k] = [send(ps_s.at[k], ps_x.at[k, n], px_s.at[k, n], px_r.at[k, n], x_peers[n]) for n in range(3)]

    def after_px(k):
        for copy in pxs[k]:
            copy.wait_recv()
        ps_t[k] = (ps_s[k] + ps_x[k, 0]) + (ps_x[k, 1] + ps_x[k, 2])
        pys[k] = [send(ps_t.at[k], ps_y.at[k, n], py_s.at[k, n], py_r.at[k, n], y_peers[n]) for n in range(3)]

    def after_py(k):
        for copy in pys[k]:
            copy.wait_recv()
        if k == 0:
            for copy in far:
                copy.wait_recv()
        sums = (ps_t[k] + ps_y[k, 0]) + (ps_y[k, 1] + ps_y[k, 2])
        inv_rms = lax.rsqrt(sums[:, 0:1] / model_width + EPS)
        cross = sums[:, 64:65] / model_width
        scale = inv_rms * inv_rms * inv_rms * cross
        mine, theirs = swap_s[k], swap_r[k]
        layer = jnp.where(sec == 0, mine, theirs)
        total = jnp.where(sec == 0, theirs, mine)
        gain_f = gv[...].astype(F32)
        other = far_resid[k].reshape(2 * tokens, 2 * half).astype(F32)
        normed = layer * inv_rms * gain_f
        grad_in = other + inv_rms * gain_f * total - layer * scale
        value = jnp.where(sec == 0, grad_in, normed).astype(BF16)
        x_[k, 0, gz1, gz0, core] = value[:, :half]
        x_[k, 1, gz1, gz0, core] = value[:, half:]
        for s, peer in enumerate((z_low, z_high)):
            part = x_.at[k, s, gz1, gz0, core]
            x1[k, s] = send(part, part, x1_s.at[k, s], x1_r.at[k, s], peer)

    def after_x1(k):
        parts = (x_.at[k, 0, gz1, :, core], x_.at[k, 1, :, gz0, core])
        for s, peer in enumerate((z_high, z_low)):
            x1[k, s].wait_recv()
            x2[k, s] = send(parts[s], parts[s], x2_s.at[k, s], x2_r.at[k, s], peer)

    def after_x2(k):
        for s in range(2):
            x2[k, s].wait_recv()
        part = x_.at[k, :, :, :, core]
        xc[k] = send(part, part, xc_s.at[k], xc_r.at[k], core_peer)

    def rs_index(q, i, value):
        done = {(q + 3 - n) % 4 for n in range(i)}
        now = (q + 3 - i) % 4
        return tuple(value if d == now else bits[d] if d in done else ALL for d in range(4)), now

    def rs_send(k, q, i):
        now = (q + 3 - i) % 4
        index, _ = rs_index(q, i, 1 - bits[now])
        rs[k, q, i] = send(p2.at[(k, q) + index], rest[i].at[k, q], rs_s.at[k, q, i], rs_r.at[k, q, i], flips[now])

    def second(k):
        xc[k].wait_recv()
        for q in range(Q):

            def tile(a, q=q):
                acc = None
                for s in range(2):
                    lhs = x_[k, s, a].reshape(8 * tokens, half)
                    rhs = w[pl.ds(q * width, width), s * half : (s + 1) * half]
                    term = lax.dot_general(lhs, rhs, (((1,), (1,)), ((), ())), preferred_element_type=F32)
                    acc = term if acc is None else acc + term
                p2[k, q, a] = acc.astype(BF16).reshape(2, 2, 2, tokens, width)

            pl.loop(0, 2)(tile)
            rs_send(k, q, 0)

    def rs_step(k, i):
        for q in range(Q):
            now = (q + 3 - i) % 4
            rs[k, q, i].wait_recv()
            index, _ = rs_index(q, i, bits[now])
            index = (k, q) + index
            total = p2[index].astype(F32) + rest[i][k, q].astype(F32)
            if i < 3:
                p2[index] = total.astype(BF16)
                rs_send(k, q, i + 1)
            else:
                outv[pl.ds(k * tokens, tokens), pl.ds(q * width, width)] = total.astype(BF16)

    def weight_grads(q):
        lhs = h[q].reshape(K * 16 * tokens, width)
        for s in range(2):
            rhs = x_[:, s].reshape(K * 16 * tokens, half)
            value = lax.dot_general(lhs, rhs, (((0,), (0,)), ((), ())), preferred_element_type=F32)
            grads[0, pl.ds(q * width, width), s * half : (s + 1) * half] = value.astype(BF16)

    for i in range(4):
        ag_send(0, i)
    far = [
        send(resid.at[0, pl.ds(start + k * tokens, tokens), :], far_resid.at[k, b], q_s.at[k, b], q_r.at[k, b], sec_peer)
        for k in range(K)
        for b, start in enumerate((start0, start1))
    ]
    ag_send(1, 0)
    ag_done(0)
    first(0)
    ag_send(1, 1)
    ag_send(1, 2)
    after_core(0)
    ag_send(1, 3)
    after_z1(0)
    after_z2(0)
    after_swap(0)
    after_px(0)
    after_py(0)
    after_x1(0)
    ag_done(1)
    first(1)
    after_x2(0)
    after_core(1)
    second(0)
    after_z1(1)
    after_z2(1)
    after_swap(1)
    after_px(1)
    after_py(1)
    rs_step(0, 0)
    after_x1(1)
    rs_step(0, 1)
    after_x2(1)
    rs_step(0, 2)
    second(1)
    rs_step(0, 3)
    weight_grads(0)
    weight_grads(1)
    rs_step(1, 0)
    weight_grads(2)
    rs_step(1, 1)
    weight_grads(3)
    rs_step(1, 2)
    rs_step(1, 3)
    final = load(outv, out.at[0], l_o)
    for copy in sends:
        copy.wait_send()
    final.wait()


def local(section_hidden, section_weight, resid_in, norm_gain):
    _, rows, units = section_hidden.shape
    _, _, features = section_weight.shape
    tokens, width, half = rows // K, units // Q, features // 2
    model_width = features * lax.axis_size("row")
    vmem, dma = pltpu.VMEM, pltpu.SemaphoreType.DMA
    cube = (2, 2, 2, 2)
    scratch = [
        vmem((units, features), BF16),
        vmem((Q, K) + cube + (tokens, width), BF16),
        vmem((K, 2, 2, 2, 2, 2 * tokens, half), F32),
        vmem((K, 2, 2, 2, 2 * tokens, half), F32),
        vmem((K, 2, 2, 2 * tokens, half), F32),
        vmem((K, 2, 2 * tokens, half), F32),
        vmem((K, 2, tokens, features), BF16),
        vmem((K, 2, tokens, features), BF16),
        vmem((K, 2 * tokens, features), F32),
        vmem((K, 2 * tokens, features), F32),
        vmem((K, 2 * tokens, 128), F32),
        vmem((K, 3, 2 * tokens, 128), F32),
        vmem((K, 2 * tokens, 128), F32),
        vmem((K, 3, 2 * tokens, 128), F32),
        vmem((K, 2, 2, 2, 2, 2 * tokens, half), BF16),
        vmem((K, Q) + cube + (tokens, width), BF16),
        vmem((K, Q, 2, 2, 2, tokens, width), BF16),
        vmem((K, Q, 2, 2, tokens, width), BF16),
        vmem((K, Q, 2, tokens, width), BF16),
        vmem((K, Q, tokens, width), BF16),
        vmem((rows, units), BF16),
        vmem((1, features), BF16),
        dma, dma((K, Q)), dma((K, 2)), dma, dma,
    ]
    for shape in ((K, Q, 4), (K, Q, 4), (K,), (K, 2), (K, 2), (K, 2), (K,), (K, 3), (K, 3), (K, 2), (K, 2), (K,)):
        scratch += [dma(shape), dma(shape)]
    hbm = pl.BlockSpec(memory_space=pl.ANY)
    flops = 3 * 2 * rows * 16 * units * features
    return pl.pallas_call(
        functools.partial(kernel, float(model_width)),
        out_shape=(
            jax.ShapeDtypeStruct((1, units, features), BF16),
            jax.ShapeDtypeStruct((1, rows, units), BF16),
        ),
        in_specs=[hbm] * 4,
        out_specs=(pl.BlockSpec(memory_space=pltpu.VMEM), hbm),
        scratch_shapes=scratch,
        compiler_params=pltpu.CompilerParams(collective_id=0, has_side_effects=True, vmem_limit_bytes=60 * 2**20),
        cost_estimate=pl.CostEstimate(flops=flops, bytes_accessed=10 * units * features, transcendentals=0),
    )(section_hidden, section_weight, resid_in, norm_gain.reshape(1, features))


def solution(mesh):
    in_specs = (
        P("section", "row", "col"),
        P("section", "col", "row"),
        P("section", "col", "row"),
        P("row"),
    )
    out_specs = (P("section", "col", "row"), P("section", "row", "col"))
    return jax.shard_map(local, mesh=mesh, in_specs=in_specs, out_specs=out_specs, check_vma=False)
```

```python
import functools

import jax
import jax.numpy as jnp
from jax import lax
from jax.experimental import pallas as pl
from jax.experimental.pallas import tpu as pltpu
from jax.sharding import PartitionSpec as P

EPS = 1e-05
MESH = pl.DeviceIdType.MESH
F32 = jnp.float32
BF16 = jnp.bfloat16
K = 4
Q = 4
ALL = slice(None)

ORDER = (0, 1, 2, 3, 0, 2, 1, 3, 0, 1, 3, 0, 2, 1, 0, 2, 3, 0, 1, 0, 1, 2, 2, 0, 3, 1, 3, 0, 1, 2, 0, 3, 1, 2, 0, 3, 1, 2, 0, 3, 1, 0, 2, 3, 1, 2, 1, 3, 2, 0, 2, 3, 3, 1, 2, 3, 1, 2, 0, 3, 2, 0, 1, 3, 0, 2, 1, 3)
FAR_AT = 10


def mask_of(pos, mask):
    if mask == 0:
        return pos
    if mask == 1:
        return pos + 1 - 2 * lax.rem(pos, 2)
    if mask == 3:
        return 3 - pos
    return lax.rem(pos + 2, 4)


def gray(pos):
    high = lax.div(pos, 2)
    low = lax.rem(pos, 2)
    return high, high + low - 2 * high * low


def kernel(model_width, hidden, weight, resid, gain, grads, out, *scratch):
    (w, h, z, rc, rz1, rz2, own_resid, far_resid, swap_s, swap_r, ps_s, ps_x, x_, own, t0, t1, t2, t3, r0, r1, r2, r3,
     outv, gv, l_w, l_h, l_r, l_o, l_g,
     ag_s, ag_r, rs_s, rs_r, zc_s, zc_r, z1_s, z1_r, z2_s, z2_r, q_s, q_r, sw_s, sw_r, px_s, px_r,
     x1_s, x1_r, x2_s, x2_r, xc_s, xc_r) = scratch
    rest = [r0, r1, r2, r3]
    away = [t0, t1, t2, t3]
    tokens = hidden.shape[1] // K
    width = hidden.shape[2] // Q
    half = weight.shape[2] // 2
    sec = lax.axis_index("section")
    row = lax.axis_index("row")
    col = lax.axis_index("col")
    px, py = lax.div(row, 4), lax.rem(row, 4)
    zh, core = lax.div(col, 2), lax.rem(col, 2)
    gx1, gx0 = gray(px)
    gy1, gy0 = gray(py)
    gz1, gz0 = gray(zh)
    bits = [gx1, gx0, gy1, gy0]
    flips = [
        {"row": mask_of(px, 3) * 4 + py},
        {"row": mask_of(px, 1) * 4 + py},
        {"row": px * 4 + mask_of(py, 3)},
        {"row": px * 4 + mask_of(py, 1)},
    ]
    row_peers = [{"row": mask_of(px, m // 4) * 4 + mask_of(py, m % 4)} for m in range(1, 16)]
    core_peer = {"col": zh * 2 + 1 - core}
    z_low = {"col": mask_of(zh, 1) * 2 + core}
    z_high = {"col": mask_of(zh, 3) * 2 + core}
    sec_peer = {"section": 1 - sec}

    barrier = pltpu.get_barrier_semaphore()
    partners = row_peers + [core_peer, z_low, z_high, sec_peer]
    for peer in partners:
        pl.semaphore_signal(barrier, inc=1, device_id=peer, device_id_type=MESH)

    loads = []

    def load(src, dst, sem):
        copy = pltpu.make_async_copy(src, dst, sem)
        copy.start()
        return copy

    def own_block(k, q):
        return hidden.at[0, pl.ds(k * tokens, tokens), pl.ds(q * width, width)]

    h_loads = [[load(own_block(k, q), h.at[q, k, gx1, gx0, gy1, gy0], l_h.at[k, q]) for q in range(Q)] for k in range(K)]
    g_load = load(gain, gv, l_g)
    w_load = load(weight.at[0], w, l_w)
    start0 = pl.multiple_of(64 * core, 64)
    start1 = pl.multiple_of(64 * (1 - core), 64)
    r_loads = [
        [load(resid.at[0, pl.ds(start + k * tokens, tokens), :], own_resid.at[k, b], l_r.at[k, b]) for b, start in enumerate((start0, start1))]
        for k in range(K)
    ]

    pl.semaphore_wait(barrier, len(partners))

    lane = lax.broadcasted_iota(jnp.int32, (2 * tokens, 128), 1)
    token = lax.broadcasted_iota(jnp.int32, (2 * tokens, 128), 0)
    at_square, at_cross = lane == token, lane == token + 2 * tokens

    sends = []

    def send(src, dst, ssem, rsem, peer):
        copy = pltpu.make_async_remote_copy(src, dst, ssem, rsem, device_id=peer, device_id_type=MESH)
        copy.start()
        sends.append(copy)
        return copy

    ag = {}

    def ag_index(q, i):
        free = {(q + n) % 4 for n in range(i)}
        return tuple(ALL if d in free else bits[d] for d in range(4))

    def ag_send(k, i):
        for q in range(Q):
            if i > 0:
                ag[k, q, i - 1].wait_recv()
            if i == 1:
                h_loads[k][q].wait()
            index = (q, k) + ag_index(q, i)
            src = own_block(k, q) if i == 0 else h.at[index]
            ag[k, q, i] = send(src, h.at[index], ag_s.at[k, q, i], ag_r.at[k, q, i], flips[(q + i) % 4])

    def ag_done(k):
        for q in range(Q):
            ag[k, q, 3].wait_recv()

    zc, z1, z2, sw, pxs, x1, x2, xc, rs = {}, {}, {}, {}, {}, {}, {}, {}, {}

    def first(k):
        if k == 0:
            w_load.wait()

        acc = None
        for q in range(Q):
            lhs = h[q, k].reshape(16 * tokens, width)
            term = jnp.dot(lhs, w[pl.ds(q * width, width), :], preferred_element_type=F32)
            acc = term if acc is None else acc + term
        for s in range(2):
            z[k, s] = acc[:, s * half : (s + 1) * half].reshape(2, 2, 2, 2 * tokens, half)
        zc[k] = send(z.at[k, :, :, :, 1 - core], rc.at[k], zc_s.at[k], zc_r.at[k], core_peer)

    def after_core(k):
        zc[k].wait_recv()
        z[k, :, :, :, core] = z[k, :, :, :, core] + rc[k]
        z1[k] = [
            send(z.at[k, 0, :, 1 - gz0, core], rz1.at[k, 0], z1_s.at[k, 0], z1_r.at[k, 0], z_low),
            send(z.at[k, 1, 1 - gz1, :, core], rz1.at[k, 1], z1_s.at[k, 1], z1_r.at[k, 1], z_high),
        ]

    def after_z1(k):
        z1[k][0].wait_recv()
        z[k, 0, :, gz0, core] = z[k, 0, :, gz0, core] + rz1[k, 0]
        first_half = send(z.at[k, 0, 1 - gz1, gz0, core], rz2.at[k, 0], z2_s.at[k, 0], z2_r.at[k, 0], z_high)
        z1[k][1].wait_recv()
        z[k, 1, gz1, :, core] = z[k, 1, gz1, :, core] + rz1[k, 1]
        z2[k] = [first_half, send(z.at[k, 1, gz1, 1 - gz0, core], rz2.at[k, 1], z2_s.at[k, 1], z2_r.at[k, 1], z_low)]

    def after_z2(k):
        for b in range(2):
            r_loads[k][b].wait()
        for s in range(2):
            z2[k][s].wait_recv()
            total = z[k, s, gz1, gz0, core] + rz2[k, s]
            res = own_resid[k, :, :, s * half : (s + 1) * half].reshape(2 * tokens, half).astype(F32)
            layer = (res + total).astype(BF16).astype(F32)
            swap_s[k, :, s * half : (s + 1) * half] = jnp.where(sec == 0, layer, total)
        sw[k] = send(swap_s.at[k], swap_r.at[k], sw_s.at[k], sw_r.at[k], sec_peer)

    def after_swap(k):
        if k == 0:
            g_load.wait()
        sw[k].wait_recv()
        mine, theirs = swap_s[k], swap_r[k]
        layer = jnp.where(sec == 0, mine, theirs)
        total = jnp.where(sec == 0, theirs, mine)
        gain_f = gv[...].astype(F32)
        squares = jnp.sum(layer * layer, axis=1, keepdims=True)
        cross = jnp.sum(total * gain_f * layer, axis=1, keepdims=True)
        line = jnp.where(at_square, squares, 0.0) + jnp.where(at_cross, cross, 0.0)
        ps_s[k] = jnp.sum(line, axis=0, keepdims=True)
        pxs[k] = [send(ps_s.at[k], ps_x.at[k, n], px_s.at[k, n], px_r.at[k, n], row_peers[n]) for n in range(15)]

    def after_sums(k):
        for copy in pxs[k]:
            copy.wait_recv()
        if k == 0:
            for copy in far:
                copy.wait_recv()
        line = ps_s[k] + jnp.sum(ps_x[k], axis=0)
        squares = jnp.sum(jnp.where(at_square, line, 0.0), axis=1, keepdims=True)
        cross = jnp.sum(jnp.where(at_cross, line, 0.0), axis=1, keepdims=True) / model_width
        inv_rms = lax.rsqrt(squares / model_width + EPS)
        scale = inv_rms * inv_rms * inv_rms * cross
        mine, theirs = swap_s[k], swap_r[k]
        layer = jnp.where(sec == 0, mine, theirs)
        total = jnp.where(sec == 0, theirs, mine)
        gain_f = gv[...].astype(F32)
        other = far_resid[k].reshape(2 * tokens, 2 * half).astype(F32)
        normed = layer * inv_rms * gain_f
        grad_in = other + inv_rms * gain_f * total - layer * scale
        value = jnp.where(sec == 0, grad_in, normed).astype(BF16)
        x_[k, 0, gz1, gz0, core] = value[:, :half]
        x_[k, 1, gz1, gz0, core] = value[:, half:]
        for s, peer in enumerate((z_low, z_high)):
            part = x_.at[k, s, gz1, gz0, core]
            x1[k, s] = send(part, part, x1_s.at[k, s], x1_r.at[k, s], peer)

    def after_x1(k):
        parts = (x_.at[k, 0, gz1, :, core], x_.at[k, 1, :, gz0, core])
        for s, peer in enumerate((z_high, z_low)):
            x1[k, s].wait_recv()
            x2[k, s] = send(parts[s], parts[s], x2_s.at[k, s], x2_r.at[k, s], peer)

    def after_x2(k):
        for s in range(2):
            x2[k, s].wait_recv()
        part = x_.at[k, :, :, :, core]
        xc[k] = send(part, part, xc_s.at[k], xc_r.at[k], core_peer)

    def rs_dim(q, i):
        return (q + 3 - i) % 4

    def rs_left(q, i):
        return [d for d in range(4) if d not in {rs_dim(q, n) for n in range(i)}]

    def split(value, q, i):
        axis = rs_left(q, i).index(rs_dim(q, i))
        low, high = (lax.index_in_dim(value, n, axis, keepdims=False) for n in range(2))
        mine = bits[rs_dim(q, i)] == 0
        return jnp.where(mine, low, high), jnp.where(mine, high, low)

    def rs_send(k, q, i):
        rs[k, q, i] = send(away[i].at[k, q], rest[i].at[k, q], rs_s.at[k, q, i], rs_r.at[k, q, i], flips[rs_dim(q, i)])

    def store(k, q, i, value):
        stays, goes = split(value, q, i)
        away[i][k, q] = goes.astype(BF16)
        rs_send(k, q, i)
        own[(k, q) + (ALL,) * (3 - i) + (0,) * i] = stays

    def second(k):
        xc[k].wait_recv()
        for q in range(Q):
            acc = None
            for s in range(2):
                lhs = x_[k, s].reshape(16 * tokens, half)
                rhs = w[pl.ds(q * width, width), s * half : (s + 1) * half]
                term = lax.dot_general(lhs, rhs, (((1,), (1,)), ((), ())), preferred_element_type=F32)
                acc = term if acc is None else acc + term
            store(k, q, 0, acc.reshape(2, 2, 2, 2, tokens, width))

    def rs_step(k, i):
        for q in range(Q):
            rs[k, q, i].wait_recv()
            total = own[(k, q) + (ALL,) * (3 - i) + (0,) * i] + rest[i][k, q].astype(F32)
            if i < 3:
                store(k, q, i + 1, total)
            else:
                outv[pl.ds(k * tokens, tokens), pl.ds(q * width, width)] = total.astype(BF16)

    def weight_grads(q):
        lhs = h[q].reshape(K * 16 * tokens, width)
        for s in range(2):
            rhs = x_[:, s].reshape(K * 16 * tokens, half)
            value = lax.dot_general(lhs, rhs, (((0,), (0,)), ((), ())), preferred_element_type=F32)
            grads[0, pl.ds(q * width, width), s * half : (s + 1) * half] = value.astype(BF16)

    far = []

    def far_send(k):
        for b, start in enumerate((start0, start1)):
            src = resid.at[0, pl.ds(start + k * tokens, tokens), :]
            far.append(send(src, far_resid.at[k, b], q_s.at[k, b], q_r.at[k, b], sec_peer))

    def stage(k, n):
        if n < 4:
            ag_send(k, n)
        elif n == 4:
            ag_done(k)
            first(k)
        elif n < 12:
            (after_core, after_z1, after_z2, after_swap, after_sums, after_x1, after_x2)[n - 5](k)
        elif n == 12:
            second(k)
        else:
            rs_step(k, n - 13)

    far = []

    def far_send(k):
        for b, start in enumerate((start0, start1)):
            src = resid.at[0, pl.ds(start + k * tokens, tokens), :]
            far.append(send(src, far_resid.at[k, b], q_s.at[k, b], q_r.at[k, b], sec_peer))

    at = [0] * K
    left = list(range(Q))
    for place, k in enumerate(ORDER):
        stage(k, at[k])
        at[k] += 1
        if place == FAR_AT:
            for c in range(K):
                far_send(c)
        if min(at) >= 13 and left:
            weight_grads(left.pop(0))
    for q in left:
        weight_grads(q)
    final = load(outv, out.at[0], l_o)
    for copy in sends:
        copy.wait_send()
    final.wait()


def local(section_hidden, section_weight, resid_in, norm_gain):
    _, rows, units = section_hidden.shape
    _, _, features = section_weight.shape
    tokens, width, half = rows // K, units // Q, features // 2
    model_width = features * lax.axis_size("row")
    vmem, dma = pltpu.VMEM, pltpu.SemaphoreType.DMA
    cube = (2, 2, 2, 2)
    scratch = [
        vmem((units, features), BF16),
        vmem((Q, K) + cube + (tokens, width), BF16),
        vmem((K, 2, 2, 2, 2, 2 * tokens, half), F32),
        vmem((K, 2, 2, 2, 2 * tokens, half), F32),
        vmem((K, 2, 2, 2 * tokens, half), F32),
        vmem((K, 2, 2 * tokens, half), F32),
        vmem((K, 2, tokens, features), BF16),
        vmem((K, 2, tokens, features), BF16),
        vmem((K, 2 * tokens, features), F32),
        vmem((K, 2 * tokens, features), F32),
        vmem((K, 1, 128), F32),
        vmem((K, 15, 1, 128), F32),
        vmem((K, 2, 2, 2, 2, 2 * tokens, half), BF16),
        vmem((K, Q, 2, 2, 2, tokens, width), F32),
        vmem((K, Q, 2, 2, 2, tokens, width), BF16),
        vmem((K, Q, 2, 2, tokens, width), BF16),
        vmem((K, Q, 2, tokens, width), BF16),
        vmem((K, Q, tokens, width), BF16),
        vmem((K, Q, 2, 2, 2, tokens, width), BF16),
        vmem((K, Q, 2, 2, tokens, width), BF16),
        vmem((K, Q, 2, tokens, width), BF16),
        vmem((K, Q, tokens, width), BF16),
        vmem((rows, units), BF16),
        vmem((1, features), BF16),
        dma, dma((K, Q)), dma((K, 2)), dma, dma,
    ]
    for shape in ((K, Q, 4), (K, Q, 4), (K,), (K, 2), (K, 2), (K, 2), (K,), (K, 15), (K, 2), (K, 2), (K,)):
        scratch += [dma(shape), dma(shape)]
    hbm = pl.BlockSpec(memory_space=pl.ANY)
    flops = 3 * 2 * rows * 16 * units * features
    return pl.pallas_call(
        functools.partial(kernel, float(model_width)),
        out_shape=(
            jax.ShapeDtypeStruct((1, units, features), BF16),
            jax.ShapeDtypeStruct((1, rows, units), BF16),
        ),
        in_specs=[hbm] * 4,
        out_specs=(pl.BlockSpec(memory_space=pltpu.VMEM), hbm),
        scratch_shapes=scratch,
        compiler_params=pltpu.CompilerParams(collective_id=0, has_side_effects=True, vmem_limit_bytes=60 * 2**20),
        cost_estimate=pl.CostEstimate(flops=flops, bytes_accessed=10 * units * features, transcendentals=0),
    )(section_hidden, section_weight, resid_in, norm_gain.reshape(1, features))


def solution(mesh):
    in_specs = (
        P("section", "row", "col"),
        P("section", "col", "row"),
        P("section", "col", "row"),
        P("row"),
    )
    out_specs = (P("section", "col", "row"), P("section", "row", "col"))
    return jax.shard_map(local, mesh=mesh, in_specs=in_specs, out_specs=out_specs, check_vma=False)
```

```python
import functools

import jax
import jax.numpy as jnp
from jax import lax
from jax.experimental import pallas as pl
from jax.experimental.pallas import tpu as pltpu
from jax.sharding import PartitionSpec as P

EPS = 1e-05
MESH = pl.DeviceIdType.MESH
F32 = jnp.float32
BF16 = jnp.bfloat16
K = 4
Q = 4
ALL = slice(None)

ORDER = (1, 3, 0, 2, 1, 3, 0, 2, 1, 0, 1, 2, 0, 1, 1, 2, 3, 0, 1, 0, 2, 1, 3, 2, 0, 1, 2, 0, 3, 1, 3, 0, 1, 2, 3, 1, 0, 2, 1, 3, 0, 2, 3, 0, 1, 2, 0, 3, 2, 1, 3, 2, 3, 0, 3, 1, 2, 3, 0, 2, 3, 2, 1, 0, 3, 2, 0, 3)
FAR_AT = 10


def mask_of(pos, mask):
    if mask == 0:
        return pos
    if mask == 1:
        return pos + 1 - 2 * lax.rem(pos, 2)
    if mask == 3:
        return 3 - pos
    return lax.rem(pos + 2, 4)


def gray(pos):
    high = lax.div(pos, 2)
    low = lax.rem(pos, 2)
    return high, high + low - 2 * high * low


def kernel(model_width, hidden, weight, resid, gain, grads, out, *scratch):
    (w, h, z, rc, rz1, rz2, own_resid, far_resid, swap_s, swap_r, ps_s, ps_x, x_, own, t0, t1, t2, t3, r0, r1, r2, r3,
     gv, l_w, l_h, l_r, l_g,
     ag_s, ag_r, rs_s, rs_r, zc_s, zc_r, z1_s, z1_r, z2_s, z2_r, q_s, q_r, sw_s, sw_r, px_s, px_r,
     x1_s, x1_r, x2_s, x2_r, xc_s, xc_r) = scratch
    rest = [r0, r1, r2, r3]
    away = [t0, t1, t2, t3]
    tokens = hidden.shape[1] // K
    width = hidden.shape[2] // Q
    half = weight.shape[2] // 2
    sec = lax.axis_index("section")
    row = lax.axis_index("row")
    col = lax.axis_index("col")
    px, py = lax.div(row, 4), lax.rem(row, 4)
    zh, core = lax.div(col, 2), lax.rem(col, 2)
    gx1, gx0 = gray(px)
    gy1, gy0 = gray(py)
    gz1, gz0 = gray(zh)
    bits = [gx1, gx0, gy1, gy0]
    flips = [
        {"row": mask_of(px, 3) * 4 + py},
        {"row": mask_of(px, 1) * 4 + py},
        {"row": px * 4 + mask_of(py, 3)},
        {"row": px * 4 + mask_of(py, 1)},
    ]
    row_peers = [{"row": mask_of(px, m // 4) * 4 + mask_of(py, m % 4)} for m in range(1, 16)]
    core_peer = {"col": zh * 2 + 1 - core}
    z_low = {"col": mask_of(zh, 1) * 2 + core}
    z_high = {"col": mask_of(zh, 3) * 2 + core}
    sec_peer = {"section": 1 - sec}

    barrier = pltpu.get_barrier_semaphore()
    partners = flips + [core_peer, z_low, z_high, sec_peer]
    for peer in partners:
        pl.semaphore_signal(barrier, inc=1, device_id=peer, device_id_type=MESH)

    loads = []

    def load(src, dst, sem):
        copy = pltpu.make_async_copy(src, dst, sem)
        copy.start()
        return copy

    def own_block(k, q):
        return hidden.at[0, pl.ds(k * tokens, tokens), pl.ds(q * width, width)]

    h_loads = [[load(own_block(k, q), h.at[q, k, gx1, gx0, gy1, gy0], l_h.at[k, q]) for q in range(Q)] for k in range(K)]
    g_load = load(gain, gv, l_g)
    w_load = load(weight.at[0], w, l_w)
    start0 = pl.multiple_of(64 * core, 64)
    start1 = pl.multiple_of(64 * (1 - core), 64)
    r_loads = [
        [load(resid.at[0, pl.ds(start + k * tokens, tokens), :], own_resid.at[k, b], l_r.at[k, b]) for b, start in enumerate((start0, start1))]
        for k in range(K)
    ]

    pl.semaphore_wait(barrier, len(partners))

    lane = lax.broadcasted_iota(jnp.int32, (2 * tokens, 128), 1)
    token = lax.broadcasted_iota(jnp.int32, (2 * tokens, 128), 0)
    at_square, at_cross = lane == token, lane == token + 2 * tokens

    sends = []

    def send(src, dst, ssem, rsem, peer):
        copy = pltpu.make_async_remote_copy(src, dst, ssem, rsem, device_id=peer, device_id_type=MESH)
        copy.start()
        sends.append(copy)
        return copy

    ag = {}

    def ag_index(q, i):
        free = {(q + n) % 4 for n in range(i)}
        return tuple(ALL if d in free else bits[d] for d in range(4))

    def ag_send(k, i):
        for q in range(Q):
            if i > 0:
                ag[k, q, i - 1].wait_recv()
            if i == 1:
                h_loads[k][q].wait()
            index = (q, k) + ag_index(q, i)
            src = own_block(k, q) if i == 0 else h.at[index]
            ag[k, q, i] = send(src, h.at[index], ag_s.at[k, q, i], ag_r.at[k, q, i], flips[(q + i) % 4])

    def ag_done(k):
        for q in range(Q):
            ag[k, q, 3].wait_recv()

    waited = set()

    def once(wait):
        if wait not in waited:
            waited.add(wait)
            wait()

    zc, z1, z2, sw, pxs, x1, x2, xc, rs = {}, {}, {}, {}, {}, {}, {}, {}, {}

    def first(k):
        once(w_load.wait)

        acc = None
        for q in range(Q):
            lhs = h[q, k].reshape(16 * tokens, width)
            term = jnp.dot(lhs, w[pl.ds(q * width, width), :], preferred_element_type=F32)
            acc = term if acc is None else acc + term
        for s in range(2):
            z[k, s] = acc[:, s * half : (s + 1) * half].reshape(2, 2, 2, 2 * tokens, half)
        zc[k] = send(z.at[k, :, :, :, 1 - core], rc.at[k], zc_s.at[k], zc_r.at[k], core_peer)

    def after_core(k):
        zc[k].wait_recv()
        z[k, :, :, :, core] = z[k, :, :, :, core] + rc[k]
        z1[k] = [
            send(z.at[k, 0, :, 1 - gz0, core], rz1.at[k, 0], z1_s.at[k, 0], z1_r.at[k, 0], z_low),
            send(z.at[k, 1, 1 - gz1, :, core], rz1.at[k, 1], z1_s.at[k, 1], z1_r.at[k, 1], z_high),
        ]

    def after_z1(k):
        z1[k][0].wait_recv()
        z[k, 0, :, gz0, core] = z[k, 0, :, gz0, core] + rz1[k, 0]
        first_half = send(z.at[k, 0, 1 - gz1, gz0, core], rz2.at[k, 0], z2_s.at[k, 0], z2_r.at[k, 0], z_high)
        z1[k][1].wait_recv()
        z[k, 1, gz1, :, core] = z[k, 1, gz1, :, core] + rz1[k, 1]
        z2[k] = [first_half, send(z.at[k, 1, gz1, 1 - gz0, core], rz2.at[k, 1], z2_s.at[k, 1], z2_r.at[k, 1], z_low)]

    def after_z2(k):
        for b in range(2):
            r_loads[k][b].wait()
        for s in range(2):
            z2[k][s].wait_recv()
            total = z[k, s, gz1, gz0, core] + rz2[k, s]
            res = own_resid[k, :, :, s * half : (s + 1) * half].reshape(2 * tokens, half).astype(F32)
            layer = (res + total).astype(BF16).astype(F32)
            swap_s[k, :, s * half : (s + 1) * half] = jnp.where(sec == 0, layer, total)
        sw[k] = send(swap_s.at[k], swap_r.at[k], sw_s.at[k], sw_r.at[k], sec_peer)

    def after_swap(k):
        once(g_load.wait)
        sw[k].wait_recv()
        mine, theirs = swap_s[k], swap_r[k]
        layer = jnp.where(sec == 0, mine, theirs)
        total = jnp.where(sec == 0, theirs, mine)
        gain_f = gv[...].astype(F32).reshape(1, 2 * half)
        squares = jnp.sum(layer * layer, axis=1, keepdims=True)
        cross = jnp.sum(total * gain_f * layer, axis=1, keepdims=True)
        line = jnp.where(at_square, squares, 0.0) + jnp.where(at_cross, cross, 0.0)
        ps_s[k] = jnp.sum(line, axis=0, keepdims=True)
        pxs[k] = [send(ps_s.at[k], ps_x.at[k, n], px_s.at[k, n], px_r.at[k, n], row_peers[n]) for n in range(15)]

    def after_sums(k):
        for copy in pxs[k]:
            copy.wait_recv()
        for copy in far[k]:
            copy.wait_recv()
        line = ps_s[k] + jnp.sum(ps_x[k], axis=0)
        squares = jnp.sum(jnp.where(at_square, line, 0.0), axis=1, keepdims=True)
        cross = jnp.sum(jnp.where(at_cross, line, 0.0), axis=1, keepdims=True) / model_width
        inv_rms = lax.rsqrt(squares / model_width + EPS)
        scale = inv_rms * inv_rms * inv_rms * cross
        mine, theirs = swap_s[k], swap_r[k]
        layer = jnp.where(sec == 0, mine, theirs)
        total = jnp.where(sec == 0, theirs, mine)
        gain_f = gv[...].astype(F32).reshape(1, 2 * half)
        other = far_resid[k].reshape(2 * tokens, 2 * half).astype(F32)
        normed = layer * inv_rms * gain_f
        grad_in = other + inv_rms * gain_f * total - layer * scale
        value = jnp.where(sec == 0, grad_in, normed).astype(BF16)
        x_[k, 0, gz1, gz0, core] = value[:, :half]
        x_[k, 1, gz1, gz0, core] = value[:, half:]
        for s, peer in enumerate((z_low, z_high)):
            part = x_.at[k, s, gz1, gz0, core]
            x1[k, s] = send(part, part, x1_s.at[k, s], x1_r.at[k, s], peer)

    def after_x1(k):
        parts = (x_.at[k, 0, gz1, :, core], x_.at[k, 1, :, gz0, core])
        for s, peer in enumerate((z_high, z_low)):
            x1[k, s].wait_recv()
            x2[k, s] = send(parts[s], parts[s], x2_s.at[k, s], x2_r.at[k, s], peer)

    def after_x2(k):
        for s in range(2):
            x2[k, s].wait_recv()
        part = x_.at[k, :, :, :, core]
        xc[k] = send(part, part, xc_s.at[k], xc_r.at[k], core_peer)

    def rs_dim(q, i):
        return (q + 3 - i) % 4

    def rs_left(q, i):
        return [d for d in range(4) if d not in {rs_dim(q, n) for n in range(i)}]

    def split(value, q, i):
        axis = rs_left(q, i).index(rs_dim(q, i))
        low, high = (lax.index_in_dim(value, n, axis, keepdims=False) for n in range(2))
        mine = bits[rs_dim(q, i)] == 0
        return jnp.where(mine, low, high), jnp.where(mine, high, low)

    def rs_send(k, q, i):
        rs[k, q, i] = send(away[i].at[k, q], rest[i].at[k, q], rs_s.at[k, q, i], rs_r.at[k, q, i], flips[rs_dim(q, i)])

    def store(k, q, i, value):
        stays, goes = split(value, q, i)
        away[i][k, q] = goes.astype(BF16)
        rs_send(k, q, i)
        own[(k, q) + (ALL,) * (3 - i) + (0,) * i] = stays

    def second(k):
        xc[k].wait_recv()
        for q in range(Q):
            acc = None
            for s in range(2):
                lhs = x_[k, s].reshape(16 * tokens, half)
                rhs = w[pl.ds(q * width, width), s * half : (s + 1) * half]
                term = lax.dot_general(lhs, rhs, (((1,), (1,)), ((), ())), preferred_element_type=F32)
                acc = term if acc is None else acc + term
            store(k, q, 0, acc.reshape(2, 2, 2, 2, tokens, width))

    def rs_step(k, i):
        for q in range(Q):
            rs[k, q, i].wait_recv()
            total = own[(k, q) + (ALL,) * (3 - i) + (0,) * i] + rest[i][k, q].astype(F32)
            if i < 3:
                store(k, q, i + 1, total)
            else:
                out[0, pl.ds(k * tokens, tokens), pl.ds(q * width, width)] = total.astype(BF16)

    def weight_grads(q):
        lhs = h[q].reshape(K * 16 * tokens, width)
        for s in range(2):
            rhs = x_[:, s].reshape(K * 16 * tokens, half)
            value = lax.dot_general(lhs, rhs, (((0,), (0,)), ((), ())), preferred_element_type=F32)
            grads[0, pl.ds(q * width, width), s * half : (s + 1) * half] = value.astype(BF16)

    far = {}

    def far_send(k):
        far[k] = []
        for b, start in enumerate((start0, start1)):
            src = resid.at[0, pl.ds(start + k * tokens, tokens), :]
            far[k].append(send(src, far_resid.at[k, b], q_s.at[k, b], q_r.at[k, b], sec_peer))

    def stage(k, n):
        if n < 4:
            ag_send(k, n)
        elif n == 4:
            ag_done(k)
            first(k)
        elif n < 12:
            (after_core, after_z1, after_z2, after_swap, after_sums, after_x1, after_x2)[n - 5](k)
        elif n == 12:
            second(k)
        else:
            rs_step(k, n - 13)

    far = {}

    def far_send(k):
        far[k] = []
        for b, start in enumerate((start0, start1)):
            src = resid.at[0, pl.ds(start + k * tokens, tokens), :]
            far[k].append(send(src, far_resid.at[k, b], q_s.at[k, b], q_r.at[k, b], sec_peer))

    at = [0] * K
    left = list(range(Q))
    for place, k in enumerate(ORDER):
        stage(k, at[k])
        at[k] += 1
        if place == FAR_AT:
            for c in range(K):
                far_send(c)
        if min(at) >= 13 and left:
            weight_grads(left.pop(0))
    for q in left:
        weight_grads(q)
    for copy in sends:
        copy.wait_send()


def local(section_hidden, section_weight, resid_in, norm_gain):
    _, rows, units = section_hidden.shape
    _, _, features = section_weight.shape
    tokens, width, half = rows // K, units // Q, features // 2
    model_width = features * lax.axis_size("row")
    vmem, dma = pltpu.VMEM, pltpu.SemaphoreType.DMA
    cube = (2, 2, 2, 2)
    scratch = [
        vmem((units, features), BF16),
        vmem((Q, K) + cube + (tokens, width), BF16),
        vmem((K, 2, 2, 2, 2, 2 * tokens, half), F32),
        vmem((K, 2, 2, 2, 2 * tokens, half), F32),
        vmem((K, 2, 2, 2 * tokens, half), F32),
        vmem((K, 2, 2 * tokens, half), F32),
        vmem((K, 2, tokens, features), BF16),
        vmem((K, 2, tokens, features), BF16),
        vmem((K, 2 * tokens, features), F32),
        vmem((K, 2 * tokens, features), F32),
        vmem((K, 1, 128), F32),
        vmem((K, 15, 1, 128), F32),
        vmem((K, 2, 2, 2, 2, 2 * tokens, half), BF16),
        vmem((K, Q, 2, 2, 2, tokens, width), F32),
        vmem((K, Q, 2, 2, 2, tokens, width), BF16),
        vmem((K, Q, 2, 2, tokens, width), BF16),
        vmem((K, Q, 2, tokens, width), BF16),
        vmem((K, Q, tokens, width), BF16),
        vmem((K, Q, 2, 2, 2, tokens, width), BF16),
        vmem((K, Q, 2, 2, tokens, width), BF16),
        vmem((K, Q, 2, tokens, width), BF16),
        vmem((K, Q, tokens, width), BF16),
        vmem((features,), BF16),
        dma, dma((K, Q)), dma((K, 2)), dma,
    ]
    for shape in ((K, Q, 4), (K, Q, 4), (K,), (K, 2), (K, 2), (K, 2), (K,), (K, 15), (K, 2), (K, 2), (K,)):
        scratch += [dma(shape), dma(shape)]
    hbm = pl.BlockSpec(memory_space=pl.ANY)
    flops = 3 * 2 * rows * 16 * units * features
    return pl.pallas_call(
        functools.partial(kernel, float(model_width)),
        out_shape=(
            pltpu.VMEM((1, units, features), BF16),
            pltpu.VMEM((1, rows, units), BF16),
        ),
        in_specs=[hbm] * 4,
        out_specs=(pl.BlockSpec(memory_space=pltpu.VMEM),) * 2,
        scratch_shapes=scratch,
        compiler_params=pltpu.CompilerParams(collective_id=0, has_side_effects=True, vmem_limit_bytes=59 * 2**20),
        cost_estimate=pl.CostEstimate(flops=flops, bytes_accessed=10 * units * features, transcendentals=0),
    )(section_hidden, section_weight, resid_in, norm_gain)


def solution(mesh):
    in_specs = (
        P("section", "row", "col"),
        P("section", "col", "row"),
        P("section", "col", "row"),
        P("row"),
    )
    out_specs = (P("section", "col", "row"), P("section", "row", "col"))
    return jax.shard_map(local, mesh=mesh, in_specs=in_specs, out_specs=out_specs, check_vma=False)
```

```python
import functools

import jax
import jax.numpy as jnp
from jax import lax
from jax.experimental import pallas as pl
from jax.experimental.pallas import tpu as pltpu
from jax.sharding import PartitionSpec as P

EPS = 1e-05
MESH = pl.DeviceIdType.MESH
F32 = jnp.float32
BF16 = jnp.bfloat16
K = 4
Q = 4
ALL = slice(None)

ORDER = (0, 3, 2, 1, 0, 3, 1, 2, 0, 1, 0, 2, 1, 0, 0, 2, 3, 1, 0, 1, 2, 3, 0, 1, 2, 0, 1, 3, 2, 0, 3, 1, 2, 0, 1, 3, 2, 0, 1, 3, 0, 2, 1, 3, 1, 2, 3, 0, 2, 1, 3, 2, 3, 1, 3, 1, 2, 3, 0, 2, 3, 2, 0, 1, 3, 2, 0, 3)
FAR_AT = 10
LAG = 16


def mask_of(pos, mask):
    if mask == 0:
        return pos
    if mask == 1:
        return pos + 1 - 2 * lax.rem(pos, 2)
    if mask == 3:
        return 3 - pos
    return lax.rem(pos + 2, 4)


def gray(pos):
    high = lax.div(pos, 2)
    low = lax.rem(pos, 2)
    return high, high + low - 2 * high * low


def kernel(model_width, hidden, weight, resid, gain, grads, out, *scratch):
    (w, h, z, rc, rz1, rz2, own_resid, far_resid, swap_s, swap_r, ps_s, ps_x, x_, own, t0, t1, t2, t3, r0, r1, r2, r3,
     gv, l_w, l_h, l_r, l_g,
     ag_s, ag_r, rs_s, rs_r, zc_s, zc_r, z1_s, z1_r, z2_s, z2_r, q_s, q_r, sw_s, sw_r, px_s, px_r,
     x1_s, x1_r, x2_s, x2_r, xc_s, xc_r) = scratch
    rest = [r0, r1, r2, r3]
    away = [t0, t1, t2, t3]
    tokens = hidden.shape[1] // K
    width = hidden.shape[2] // Q
    half = weight.shape[2] // 2
    sec = lax.axis_index("section")
    row = lax.axis_index("row")
    col = lax.axis_index("col")
    px, py = lax.div(row, 4), lax.rem(row, 4)
    zh, core = lax.div(col, 2), lax.rem(col, 2)
    gx1, gx0 = gray(px)
    gy1, gy0 = gray(py)
    gz1, gz0 = gray(zh)
    bits = [gx1, gx0, gy1, gy0]
    flips = [
        {"row": mask_of(px, 3) * 4 + py},
        {"row": mask_of(px, 1) * 4 + py},
        {"row": px * 4 + mask_of(py, 3)},
        {"row": px * 4 + mask_of(py, 1)},
    ]
    row_peers = [{"row": mask_of(px, m // 4) * 4 + mask_of(py, m % 4)} for m in range(1, 16)]
    core_peer = {"col": zh * 2 + 1 - core}
    z_low = {"col": mask_of(zh, 1) * 2 + core}
    z_high = {"col": mask_of(zh, 3) * 2 + core}
    sec_peer = {"section": 1 - sec}

    barrier = pltpu.get_barrier_semaphore()
    partners = flips + [core_peer, z_low, z_high, sec_peer]
    for peer in partners:
        pl.semaphore_signal(barrier, inc=1, device_id=peer, device_id_type=MESH)

    loads = []

    def load(src, dst, sem):
        copy = pltpu.make_async_copy(src, dst, sem)
        copy.start()
        return copy

    def own_block(k, q):
        return hidden.at[0, pl.ds(k * tokens, tokens), pl.ds(q * width, width)]

    h_loads = [[load(own_block(k, q), h.at[q, k, gx1, gx0, gy1, gy0], l_h.at[k, q]) for q in range(Q)] for k in range(K)]
    g_load = load(gain, gv, l_g)
    w_load = load(weight.at[0], w, l_w)
    start0 = pl.multiple_of(64 * core, 64)
    start1 = pl.multiple_of(64 * (1 - core), 64)
    r_loads = [
        [load(resid.at[0, pl.ds(start + k * tokens, tokens), :], own_resid.at[k, b], l_r.at[k, b]) for b, start in enumerate((start0, start1))]
        for k in range(K)
    ]

    pl.semaphore_wait(barrier, len(partners))

    lane = lax.broadcasted_iota(jnp.int32, (2 * tokens, 128), 1)
    token = lax.broadcasted_iota(jnp.int32, (2 * tokens, 128), 0)
    at_square, at_cross = lane == token, lane == token + 2 * tokens

    sends = []

    class AllSent:
        def __init__(self, like, sem):
            self.wait_send = pltpu.make_async_copy(like, like, sem).wait

    def send(src, dst, ssem, rsem, peer):
        copy = pltpu.make_async_remote_copy(src, dst, ssem, rsem, device_id=peer, device_id_type=MESH)
        copy.start()
        sends.append(copy)
        return copy

    ag = {}

    def ag_index(q, i):
        free = {(q + n) % 4 for n in range(i)}
        return tuple(ALL if d in free else bits[d] for d in range(4))

    def ag_send(k, i):
        for q in range(Q):
            if i > 0:
                ag[k, q, i - 1].wait_recv()
            if i == 1:
                h_loads[k][q].wait()
            index = (q, k) + ag_index(q, i)
            src = own_block(k, q) if i == 0 else h.at[index]
            ag[k, q, i] = send(src, h.at[index], ag_s.at[k, q, i], ag_r.at[k, q, i], flips[(q + i) % 4])

    def ag_done(k):
        for q in range(Q):
            ag[k, q, 3].wait_recv()

    waited = set()

    def once(wait):
        if wait not in waited:
            waited.add(wait)
            wait()

    zc, z1, z2, sw, x1, x2, xc, rs = {}, {}, {}, {}, {}, {}, {}, {}

    def first(k):
        once(w_load.wait)

        acc = None
        for q in range(Q):
            lhs = h[q, k].reshape(16 * tokens, width)
            term = jnp.dot(lhs, w[pl.ds(q * width, width), :], preferred_element_type=F32)
            acc = term if acc is None else acc + term
        for s in range(2):
            z[k, s] = acc[:, s * half : (s + 1) * half].reshape(2, 2, 2, 2 * tokens, half)
        zc[k] = send(z.at[k, :, :, :, 1 - core], rc.at[k], zc_s.at[k], zc_r.at[k], core_peer)

    def after_core(k):
        zc[k].wait_recv()
        z[k, :, :, :, core] = z[k, :, :, :, core] + rc[k]
        z1[k] = [
            send(z.at[k, 0, :, 1 - gz0, core], rz1.at[k, 0], z1_s.at[k, 0], z1_r.at[k, 0], z_low),
            send(z.at[k, 1, 1 - gz1, :, core], rz1.at[k, 1], z1_s.at[k, 1], z1_r.at[k, 1], z_high),
        ]

    def after_z1(k):
        z1[k][0].wait_recv()
        z[k, 0, :, gz0, core] = z[k, 0, :, gz0, core] + rz1[k, 0]
        first_half = send(z.at[k, 0, 1 - gz1, gz0, core], rz2.at[k, 0], z2_s.at[k, 0], z2_r.at[k, 0], z_high)
        z1[k][1].wait_recv()
        z[k, 1, gz1, :, core] = z[k, 1, gz1, :, core] + rz1[k, 1]
        z2[k] = [first_half, send(z.at[k, 1, gz1, 1 - gz0, core], rz2.at[k, 1], z2_s.at[k, 1], z2_r.at[k, 1], z_low)]

    def after_z2(k):
        for b in range(2):
            r_loads[k][b].wait()
        for s in range(2):
            z2[k][s].wait_recv()
            total = z[k, s, gz1, gz0, core] + rz2[k, s]
            res = own_resid[k, :, :, s * half : (s + 1) * half].reshape(2 * tokens, half).astype(F32)
            layer = (res + total).astype(BF16).astype(F32)
            swap_s[k, :, s * half : (s + 1) * half] = jnp.where(sec == 0, layer, total)
        sw[k] = send(swap_s.at[k], swap_r.at[k], sw_s.at[k], sw_r.at[k], sec_peer)

    def after_swap(k):
        once(g_load.wait)
        sw[k].wait_recv()
        mine, theirs = swap_s[k], swap_r[k]
        layer = jnp.where(sec == 0, mine, theirs)
        total = jnp.where(sec == 0, theirs, mine)
        gain_f = gv[...].astype(F32).reshape(1, 2 * half)
        squares = jnp.sum(layer * layer, axis=1, keepdims=True)
        cross = jnp.sum(total * gain_f * layer, axis=1, keepdims=True)
        line = jnp.where(at_square, squares, 0.0) + jnp.where(at_cross, cross, 0.0)
        ps_s[k] = jnp.sum(line, axis=0, keepdims=True)
        for n, peer in enumerate(row_peers):
            pltpu.make_async_remote_copy(
                ps_s.at[k], ps_x.at[k, n], px_s.at[k], px_r.at[k], device_id=peer, device_id_type=MESH
            ).start()
        sends.append(AllSent(ps_x.at[k], px_s.at[k]))

    def after_sums(k):
        pltpu.make_async_copy(ps_x.at[k], ps_x.at[k], px_r.at[k]).wait()
        for copy in far[k]:
            copy.wait_recv()
        line = ps_s[k] + jnp.sum(ps_x[k], axis=0)
        squares = jnp.sum(jnp.where(at_square, line, 0.0), axis=1, keepdims=True)
        cross = jnp.sum(jnp.where(at_cross, line, 0.0), axis=1, keepdims=True) / model_width
        inv_rms = lax.rsqrt(squares / model_width + EPS)
        scale = inv_rms * inv_rms * inv_rms * cross
        mine, theirs = swap_s[k], swap_r[k]
        layer = jnp.where(sec == 0, mine, theirs)
        total = jnp.where(sec == 0, theirs, mine)
        gain_f = gv[...].astype(F32).reshape(1, 2 * half)
        other = far_resid[k].reshape(2 * tokens, 2 * half).astype(F32)
        normed = layer * inv_rms * gain_f
        grad_in = other + inv_rms * gain_f * total - layer * scale
        value = jnp.where(sec == 0, grad_in, normed).astype(BF16)
        x_[k, 0, gz1, gz0, core] = value[:, :half]
        x_[k, 1, gz1, gz0, core] = value[:, half:]
        for s, peer in enumerate((z_low, z_high)):
            part = x_.at[k, s, gz1, gz0, core]
            x1[k, s] = send(part, part, x1_s.at[k, s], x1_r.at[k, s], peer)

    def after_x1(k):
        parts = (x_.at[k, 0, gz1, :, core], x_.at[k, 1, :, gz0, core])
        for s, peer in enumerate((z_high, z_low)):
            x1[k, s].wait_recv()
            x2[k, s] = send(parts[s], parts[s], x2_s.at[k, s], x2_r.at[k, s], peer)

    def after_x2(k):
        for s in range(2):
            x2[k, s].wait_recv()
        part = x_.at[k, :, :, :, core]
        xc[k] = send(part, part, xc_s.at[k], xc_r.at[k], core_peer)

    def rs_dim(q, i):
        return (q + 3 - i) % 4

    def rs_left(q, i):
        return [d for d in range(4) if d not in {rs_dim(q, n) for n in range(i)}]

    def split(value, q, i):
        axis = rs_left(q, i).index(rs_dim(q, i))
        low, high = (lax.index_in_dim(value, n, axis, keepdims=False) for n in range(2))
        mine = bits[rs_dim(q, i)] == 0
        return jnp.where(mine, low, high), jnp.where(mine, high, low)

    def rs_send(k, q, i):
        rs[k, q, i] = send(away[i].at[k, q], rest[i].at[k, q], rs_s.at[k, q, i], rs_r.at[k, q, i], flips[rs_dim(q, i)])

    def store(k, q, i, value):
        stays, goes = split(value, q, i)
        away[i][k, q] = goes.astype(BF16)
        rs_send(k, q, i)
        own[(k, q) + (ALL,) * (3 - i) + (0,) * i] = stays

    def second(k):
        xc[k].wait_recv()
        for q in range(Q):
            acc = None
            for s in range(2):
                lhs = x_[k, s].reshape(16 * tokens, half)
                rhs = w[pl.ds(q * width, width), s * half : (s + 1) * half]
                term = lax.dot_general(lhs, rhs, (((1,), (1,)), ((), ())), preferred_element_type=F32)
                acc = term if acc is None else acc + term
            store(k, q, 0, acc.reshape(2, 2, 2, 2, tokens, width))

    def rs_step(k, i):
        for q in range(Q):
            rs[k, q, i].wait_recv()
            total = own[(k, q) + (ALL,) * (3 - i) + (0,) * i] + rest[i][k, q].astype(F32)
            if i < 3:
                store(k, q, i + 1, total)
            else:
                out[0, pl.ds(k * tokens, tokens), pl.ds(q * width, width)] = total.astype(BF16)

    def weight_grads(q):
        lhs = h[q].reshape(K * 16 * tokens, width)
        for s in range(2):
            rhs = x_[:, s].reshape(K * 16 * tokens, half)
            value = lax.dot_general(lhs, rhs, (((0,), (0,)), ((), ())), preferred_element_type=F32)
            grads[0, pl.ds(q * width, width), s * half : (s + 1) * half] = value.astype(BF16)

    def stage(k, n):
        if n < 4:
            ag_send(k, n)
        elif n == 4:
            ag_done(k)
            first(k)
        elif n < 12:
            (after_core, after_z1, after_z2, after_swap, after_sums, after_x1, after_x2)[n - 5](k)
        elif n == 12:
            second(k)
        else:
            rs_step(k, n - 13)

    far = {}

    def far_send(k):
        far[k] = []
        for b, start in enumerate((start0, start1)):
            src = resid.at[0, pl.ds(start + k * tokens, tokens), :]
            far[k].append(send(src, far_resid.at[k, b], q_s.at[k, b], q_r.at[k, b], sec_peer))

    at = [0] * K
    left = list(range(Q))
    sent, ended = [], 0
    for place, k in enumerate(ORDER):
        stage(k, at[k])
        at[k] += 1
        if place == FAR_AT:
            for c in range(K):
                far_send(c)
        if min(at) >= 13 and left:
            weight_grads(left.pop(0))
        sent.append(len(sends))
        if place >= LAG:
            while ended < sent[place - LAG]:
                sends[ended].wait_send()
                ended += 1
    for q in left:
        weight_grads(q)
    for copy in sends[ended:]:
        copy.wait_send()


def local(section_hidden, section_weight, resid_in, norm_gain):
    _, rows, units = section_hidden.shape
    _, _, features = section_weight.shape
    tokens, width, half = rows // K, units // Q, features // 2
    model_width = features * lax.axis_size("row")
    vmem, dma = pltpu.VMEM, pltpu.SemaphoreType.DMA
    cube = (2, 2, 2, 2)
    scratch = [
        vmem((units, features), BF16),
        vmem((Q, K) + cube + (tokens, width), BF16),
        vmem((K, 2, 2, 2, 2, 2 * tokens, half), F32),
        vmem((K, 2, 2, 2, 2 * tokens, half), F32),
        vmem((K, 2, 2, 2 * tokens, half), F32),
        vmem((K, 2, 2 * tokens, half), F32),
        vmem((K, 2, tokens, features), BF16),
        vmem((K, 2, tokens, features), BF16),
        vmem((K, 2 * tokens, features), F32),
        vmem((K, 2 * tokens, features), F32),
        vmem((K, 1, 128), F32),
        vmem((K, 15, 1, 128), F32),
        vmem((K, 2, 2, 2, 2, 2 * tokens, half), BF16),
        vmem((K, Q, 2, 2, 2, tokens, width), F32),
        vmem((K, Q, 2, 2, 2, tokens, width), BF16),
        vmem((K, Q, 2, 2, tokens, width), BF16),
        vmem((K, Q, 2, tokens, width), BF16),
        vmem((K, Q, tokens, width), BF16),
        vmem((K, Q, 2, 2, 2, tokens, width), BF16),
        vmem((K, Q, 2, 2, tokens, width), BF16),
        vmem((K, Q, 2, tokens, width), BF16),
        vmem((K, Q, tokens, width), BF16),
        vmem((features,), BF16),
        dma, dma((K, Q)), dma((K, 2)), dma,
    ]
    for shape in ((K, Q, 4), (K, Q, 4), (K,), (K, 2), (K, 2), (K, 2), (K,), (K,), (K, 2), (K, 2), (K,)):
        scratch += [dma(shape), dma(shape)]
    hbm = pl.BlockSpec(memory_space=pl.ANY)
    flops = 3 * 2 * rows * 16 * units * features
    return pl.pallas_call(
        functools.partial(kernel, float(model_width)),
        out_shape=(
            pltpu.VMEM((1, units, features), BF16),
            pltpu.VMEM((1, rows, units), BF16),
        ),
        in_specs=[hbm] * 4,
        out_specs=(pl.BlockSpec(memory_space=pltpu.VMEM),) * 2,
        scratch_shapes=scratch,
        compiler_params=pltpu.CompilerParams(collective_id=0, has_side_effects=True, vmem_limit_bytes=59 * 2**20),
        cost_estimate=pl.CostEstimate(flops=flops, bytes_accessed=10 * units * features, transcendentals=0),
    )(section_hidden, section_weight, resid_in, norm_gain)


def solution(mesh):
    in_specs = (
        P("section", "row", "col"),
        P("section", "col", "row"),
        P("section", "col", "row"),
        P("row"),
    )
    out_specs = (P("section", "col", "row"), P("section", "row", "col"))
    return jax.shard_map(local, mesh=mesh, in_specs=in_specs, out_specs=out_specs, check_vma=False)
```

```python
import functools

import jax
import jax.numpy as jnp
from jax import lax
from jax.experimental import pallas as pl
from jax.experimental.pallas import tpu as pltpu
from jax.sharding import PartitionSpec as P

EPS = 1e-05
MESH = pl.DeviceIdType.MESH
F32 = jnp.float32
BF16 = jnp.bfloat16
K = 4
Q = 4
ALL = slice(None)

ORDER = (2, 1, 0, 2, 3, 1, 0, 2, 1, 0, 2, 1, 2, 3, 0, 2, 1, 3, 1, 2, 0, 3, 1, 2, 0, 1, 2, 3, 0, 3, 1, 2, 0, 1, 3, 2, 0, 1, 3, 2, 0, 2, 3, 1, 0, 1, 3, 0, 2, 3, 0, 3, 1, 3, 0, 1, 3, 0, 2, 3, 1, 0, 2, 3, 0, 2, 1, 3)
FAR_AT = 10
LAG = 16


def mask_of(pos, mask):
    if mask == 0:
        return pos
    if mask == 1:
        return pos + 1 - 2 * lax.rem(pos, 2)
    if mask == 3:
        return 3 - pos
    return lax.rem(pos + 2, 4)


def gray(pos):
    high = lax.div(pos, 2)
    low = lax.rem(pos, 2)
    return high, high + low - 2 * high * low


def kernel(model_width, hidden, weight, resid, gain, grads, out, *scratch):
    (w, h, z, rc, rz1, rz2, own_resid, far_resid, swap_s, swap_r, ps_s, ps_x, x_, own, t0, t1, t2, t3, r0, r1, r2, r3,
     gv, l_w, l_h, l_r, l_g,
     ag_s, ag_r, rs_s, rs_r, zc_s, zc_r, z1_s, z1_r, z2_s, z2_r, q_s, q_r, sw_s, sw_r, px_s, px_r,
     x1_s, x1_r, x2_s, x2_r, xc_s, xc_r) = scratch
    rest = [r0, r1, r2, r3]
    away = [t0, t1, t2, t3]
    tokens = hidden.shape[1] // K
    width = hidden.shape[2] // Q
    half = weight.shape[2] // 2
    sec = lax.axis_index("section")
    row = lax.axis_index("row")
    col = lax.axis_index("col")
    px, py = lax.div(row, 4), lax.rem(row, 4)
    zh, core = lax.div(col, 2), lax.rem(col, 2)
    gx1, gx0 = gray(px)
    gy1, gy0 = gray(py)
    gz1, gz0 = gray(zh)
    bits = [gx1, gx0, gy1, gy0]
    flips = [
        {"row": mask_of(px, 3) * 4 + py},
        {"row": mask_of(px, 1) * 4 + py},
        {"row": px * 4 + mask_of(py, 3)},
        {"row": px * 4 + mask_of(py, 1)},
    ]
    row_peers = [{"row": mask_of(px, m // 4) * 4 + mask_of(py, m % 4)} for m in range(1, 16)]
    core_peer = {"col": zh * 2 + 1 - core}
    z_low = {"col": mask_of(zh, 1) * 2 + core}
    z_high = {"col": mask_of(zh, 3) * 2 + core}
    sec_peer = {"section": 1 - sec}

    barrier = pltpu.get_barrier_semaphore()
    partners = flips + [core_peer, z_low, z_high, sec_peer]
    for peer in partners:
        pl.semaphore_signal(barrier, inc=1, device_id=peer, device_id_type=MESH)

    loads = []

    def load(src, dst, sem):
        copy = pltpu.make_async_copy(src, dst, sem)
        copy.start()
        return copy

    def own_block(k, q):
        return hidden.at[0, pl.ds(k * tokens, tokens), pl.ds(q * width, width)]

    h_loads = [[load(own_block(k, q), h.at[q, k, gx1, gx0, gy1, gy0], l_h.at[k, q]) for q in range(Q)] for k in range(K)]
    g_load = load(gain, gv, l_g)
    w_load = load(weight.at[0], w, l_w)
    start0 = pl.multiple_of(64 * core, 64)
    start1 = pl.multiple_of(64 * (1 - core), 64)
    r_loads = [
        [load(resid.at[0, pl.ds(start + k * tokens, tokens), :], own_resid.at[k, b], l_r.at[k, b]) for b, start in enumerate((start0, start1))]
        for k in range(K)
    ]

    pl.semaphore_wait(barrier, len(partners))

    lane = lax.broadcasted_iota(jnp.int32, (2 * tokens, 128), 1)
    token = lax.broadcasted_iota(jnp.int32, (2 * tokens, 128), 0)
    at_square, at_cross = lane == token, lane == token + 2 * tokens

    sends = []

    class AllSent:
        def __init__(self, like, sem):
            self.wait_send = pltpu.make_async_copy(like, like, sem).wait

    def send(src, dst, ssem, rsem, peer):
        copy = pltpu.make_async_remote_copy(src, dst, ssem, rsem, device_id=peer, device_id_type=MESH)
        copy.start()
        sends.append(copy)
        return copy

    ag = {}

    def ag_index(q, i):
        free = {(q + n) % 4 for n in range(i)}
        return tuple(ALL if d in free else bits[d] for d in range(4))

    def ag_send(k, i):
        for q in range(Q):
            if i > 0:
                ag[k, q, i - 1].wait_recv()
            if i == 1:
                h_loads[k][q].wait()
            index = (q, k) + ag_index(q, i)
            src = own_block(k, q) if i == 0 else h.at[index]
            ag[k, q, i] = send(src, h.at[index], ag_s.at[k, q, i], ag_r.at[k, q, i], flips[(q + i) % 4])

    def ag_done(k):
        for q in range(Q):
            ag[k, q, 3].wait_recv()

    waited = set()

    def once(wait):
        if wait not in waited:
            waited.add(wait)
            wait()

    zc, z1, z2, sw, x1, x2, xc, rs = {}, {}, {}, {}, {}, {}, {}, {}

    def first(k):
        once(w_load.wait)

        acc = None
        for q in range(Q):
            lhs = h[q, k].reshape(16 * tokens, width)
            term = jnp.dot(lhs, w[pl.ds(q * width, width), :], preferred_element_type=F32)
            acc = term if acc is None else acc + term
        for s in range(2):
            z[k, s] = acc[:, s * half : (s + 1) * half].reshape(2, 2, 2, 2 * tokens, half)
        zc[k] = send(z.at[k, :, :, :, 1 - core], rc.at[k], zc_s.at[k], zc_r.at[k], core_peer)

    def after_core(k):
        zc[k].wait_recv()
        z[k, :, :, :, core] = z[k, :, :, :, core] + rc[k]
        z1[k] = [
            send(z.at[k, 0, :, 1 - gz0, core], rz1.at[k, 0], z1_s.at[k, 0], z1_r.at[k, 0], z_low),
            send(z.at[k, 1, 1 - gz1, :, core], rz1.at[k, 1], z1_s.at[k, 1], z1_r.at[k, 1], z_high),
        ]

    def after_z1(k):
        z1[k][0].wait_recv()
        z[k, 0, :, gz0, core] = z[k, 0, :, gz0, core] + rz1[k, 0]
        first_half = send(z.at[k, 0, 1 - gz1, gz0, core], rz2.at[k, 0], z2_s.at[k, 0], z2_r.at[k, 0], z_high)
        z1[k][1].wait_recv()
        z[k, 1, gz1, :, core] = z[k, 1, gz1, :, core] + rz1[k, 1]
        z2[k] = [first_half, send(z.at[k, 1, gz1, 1 - gz0, core], rz2.at[k, 1], z2_s.at[k, 1], z2_r.at[k, 1], z_low)]

    def after_z2(k):
        for b in range(2):
            r_loads[k][b].wait()
        for s in range(2):
            z2[k][s].wait_recv()
            total = z[k, s, gz1, gz0, core] + rz2[k, s]
            res = own_resid[k, :, :, s * half : (s + 1) * half].reshape(2 * tokens, half).astype(F32)
            layer = (res + total).astype(BF16).astype(F32)
            swap_s[k, :, s * half : (s + 1) * half] = jnp.where(sec == 0, layer, total)
        sw[k] = send(swap_s.at[k], swap_r.at[k], sw_s.at[k], sw_r.at[k], sec_peer)

    def after_swap(k):
        once(g_load.wait)
        sw[k].wait_recv()
        mine, theirs = swap_s[k], swap_r[k]
        layer = jnp.where(sec == 0, mine, theirs)
        total = jnp.where(sec == 0, theirs, mine)
        gain_f = gv[...].astype(F32).reshape(1, 2 * half)
        squares = jnp.sum(layer * layer, axis=1, keepdims=True)
        cross = jnp.sum(total * gain_f * layer, axis=1, keepdims=True)
        line = jnp.where(at_square, squares, 0.0) + jnp.where(at_cross, cross, 0.0)
        ps_s[k] = jnp.sum(line, axis=0, keepdims=True)
        for n, peer in enumerate(row_peers):
            pltpu.make_async_remote_copy(
                ps_s.at[k], ps_x.at[k, n], px_s.at[k], px_r.at[k], device_id=peer, device_id_type=MESH
            ).start()
        sends.append(AllSent(ps_x.at[k], px_s.at[k]))

    def after_sums(k):
        pltpu.make_async_copy(ps_x.at[k], ps_x.at[k], px_r.at[k]).wait()
        for copy in far[k]:
            copy.wait_recv()
        line = ps_s[k] + jnp.sum(ps_x[k], axis=0)
        squares = jnp.sum(jnp.where(at_square, line, 0.0), axis=1, keepdims=True)
        cross = jnp.sum(jnp.where(at_cross, line, 0.0), axis=1, keepdims=True) / model_width
        inv_rms = lax.rsqrt(squares / model_width + EPS)
        scale = inv_rms * inv_rms * inv_rms * cross
        mine, theirs = swap_s[k], swap_r[k]
        layer = jnp.where(sec == 0, mine, theirs)
        total = jnp.where(sec == 0, theirs, mine)
        gain_f = gv[...].astype(F32).reshape(1, 2 * half)
        other = far_resid[k].reshape(2 * tokens, 2 * half).astype(F32)
        normed = layer * inv_rms * gain_f
        grad_in = other + inv_rms * gain_f * total - layer * scale
        value = jnp.where(sec == 0, grad_in, normed).astype(BF16)
        x_[k, 0, gz1, gz0, core] = value[:, :half]
        x_[k, 1, gz1, gz0, core] = value[:, half:]
        for s, peer in enumerate((z_low, z_high)):
            part = x_.at[k, s, gz1, gz0, core]
            x1[k, s] = send(part, part, x1_s.at[k, s], x1_r.at[k, s], peer)

    def after_x1(k):
        parts = (x_.at[k, 0, gz1, :, core], x_.at[k, 1, :, gz0, core])
        for s, peer in enumerate((z_high, z_low)):
            x1[k, s].wait_recv()
            x2[k, s] = send(parts[s], parts[s], x2_s.at[k, s], x2_r.at[k, s], peer)

    def after_x2(k):
        for s in range(2):
            x2[k, s].wait_recv()
        part = x_.at[k, :, :, :, core]
        xc[k] = send(part, part, xc_s.at[k], xc_r.at[k], core_peer)

    def rs_dim(q, i):
        return (q + 3 - i) % 4

    def rs_left(q, i):
        return [d for d in range(4) if d not in {rs_dim(q, n) for n in range(i)}]

    def split(value, q, i):
        axis = rs_left(q, i).index(rs_dim(q, i))
        low, high = (lax.index_in_dim(value, n, axis, keepdims=False) for n in range(2))
        mine = bits[rs_dim(q, i)] == 0
        return jnp.where(mine, low, high), jnp.where(mine, high, low)

    def rs_send(k, q, i):
        rs[k, q, i] = send(away[i].at[k, q], rest[i].at[k, q], rs_s.at[k, q, i], rs_r.at[k, q, i], flips[rs_dim(q, i)])

    def store(k, q, i, value):
        stays, goes = split(value, q, i)
        away[i][k, q] = goes.astype(BF16)
        rs_send(k, q, i)
        own[(k, q) + (ALL,) * (3 - i) + (0,) * i] = stays

    def second(k):
        xc[k].wait_recv()
        for q in range(Q):
            acc = None
            for s in range(2):
                lhs = x_[k, s].reshape(16 * tokens, half)
                rhs = w[pl.ds(q * width, width), s * half : (s + 1) * half]
                term = lax.dot_general(lhs, rhs, (((1,), (1,)), ((), ())), preferred_element_type=F32)
                acc = term if acc is None else acc + term
            store(k, q, 0, acc.reshape(2, 2, 2, 2, tokens, width))

    def rs_step(k, i):
        for q in range(Q):
            rs[k, q, i].wait_recv()
            total = own[(k, q) + (ALL,) * (3 - i) + (0,) * i] + rest[i][k, q].astype(F32)
            if i < 3:
                store(k, q, i + 1, total)
            else:
                out[0, pl.ds(k * tokens, tokens), pl.ds(q * width, width)] = total.astype(BF16)

    def weight_grads(q):
        lhs = h[q].reshape(K * 16 * tokens, width)
        for s in range(2):
            rhs = x_[:, s].reshape(K * 16 * tokens, half)
            value = lax.dot_general(lhs, rhs, (((0,), (0,)), ((), ())), preferred_element_type=F32)
            grads[0, pl.ds(q * width, width), s * half : (s + 1) * half] = value.astype(BF16)

    def stage(k, n):
        if n < 4:
            ag_send(k, n)
        elif n == 4:
            ag_done(k)
            first(k)
        elif n < 12:
            (after_core, after_z1, after_z2, after_swap, after_sums, after_x1, after_x2)[n - 5](k)
        elif n == 12:
            second(k)
        else:
            rs_step(k, n - 13)

    far = {}

    def far_send(k):
        far[k] = []
        for b, start in enumerate((start0, start1)):
            src = resid.at[0, pl.ds(start + k * tokens, tokens), :]
            far[k].append(send(src, far_resid.at[k, b], q_s.at[k, b], q_r.at[k, b], sec_peer))

    at = [0] * K
    left = list(range(Q))
    sent, ended = [], 0
    for place, k in enumerate(ORDER):
        stage(k, at[k])
        at[k] += 1
        if place == FAR_AT:
            for c in range(K):
                far_send(c)
        if min(at) >= 13 and left:
            weight_grads(left.pop(0))
        sent.append(len(sends))
        if place >= LAG:
            while ended < sent[place - LAG]:
                sends[ended].wait_send()
                ended += 1
    for q in left:
        weight_grads(q)
    for copy in sends[ended:]:
        copy.wait_send()


def local(section_hidden, section_weight, resid_in, norm_gain):
    _, rows, units = section_hidden.shape
    _, _, features = section_weight.shape
    tokens, width, half = rows // K, units // Q, features // 2
    model_width = features * lax.axis_size("row")
    vmem, dma = pltpu.VMEM, pltpu.SemaphoreType.DMA
    cube = (2, 2, 2, 2)
    scratch = [
        vmem((units, features), BF16),
        vmem((Q, K) + cube + (tokens, width), BF16),
        vmem((K, 2, 2, 2, 2, 2 * tokens, half), F32),
        vmem((K, 2, 2, 2, 2 * tokens, half), F32),
        vmem((K, 2, 2, 2 * tokens, half), F32),
        vmem((K, 2, 2 * tokens, half), F32),
        vmem((K, 2, tokens, features), BF16),
        vmem((K, 2, tokens, features), BF16),
        vmem((K, 2 * tokens, features), F32),
        vmem((K, 2 * tokens, features), F32),
        vmem((K, 1, 128), F32),
        vmem((K, 15, 1, 128), F32),
        vmem((K, 2, 2, 2, 2, 2 * tokens, half), BF16),
        vmem((K, Q, 2, 2, 2, tokens, width), F32),
        vmem((K, Q, 2, 2, 2, tokens, width), BF16),
        vmem((K, Q, 2, 2, tokens, width), BF16),
        vmem((K, Q, 2, tokens, width), BF16),
        vmem((K, Q, tokens, width), BF16),
        vmem((K, Q, 2, 2, 2, tokens, width), BF16),
        vmem((K, Q, 2, 2, tokens, width), BF16),
        vmem((K, Q, 2, tokens, width), BF16),
        vmem((K, Q, tokens, width), BF16),
        vmem((features,), BF16),
        dma, dma((K, Q)), dma((K, 2)), dma,
    ]
    for shape in ((K, Q, 4), (K, Q, 4), (K,), (K, 2), (K, 2), (K, 2), (K,), (K,), (K, 2), (K, 2), (K,)):
        scratch += [dma(shape), dma(shape)]
    hbm = pl.BlockSpec(memory_space=pl.ANY)
    flops = 3 * 2 * rows * 16 * units * features
    return pl.pallas_call(
        functools.partial(kernel, float(model_width)),
        out_shape=(
            pltpu.VMEM((1, units, features), BF16),
            pltpu.VMEM((1, rows, units), BF16),
        ),
        in_specs=[hbm] * 4,
        out_specs=(pl.BlockSpec(memory_space=pltpu.VMEM),) * 2,
        scratch_shapes=scratch,
        compiler_params=pltpu.CompilerParams(collective_id=0, has_side_effects=True, vmem_limit_bytes=59 * 2**20),
        cost_estimate=pl.CostEstimate(flops=flops, bytes_accessed=10 * units * features, transcendentals=0),
    )(section_hidden, section_weight, resid_in, norm_gain)


def solution(mesh):
    in_specs = (
        P("section", "row", "col"),
        P("section", "col", "row"),
        P("section", "col", "row"),
        P("row"),
    )
    out_specs = (P("section", "col", "row"), P("section", "row", "col"))
    return jax.shard_map(local, mesh=mesh, in_specs=in_specs, out_specs=out_specs, check_vma=False)
```
